32 devices in a mesh: section: 2 (over x), wafer: 4 (over y, core), sub: 4 (over z).
Axes of the slice: x: 2, y: 2, z: 4, core: 2. Of those that a mesh axis runs over, the one named last changes fastest.
Arguments:
- tod: float32 [1, 256, 2048], P(None, 'wafer', ('section', 'sub')), may hold values from -6 to 6
- templates: float32 [1, 256, 2048], P(None, 'wafer', ('section', 'sub'))
- det_weight: float32 [256], P('wafer'), may hold values from 0.3 to 3
- pixel: int32 [1, 256, 2048], P(None, 'wafer', ('section', 'sub')), may hold values from 0 to 511
- hitlist: int32 [1, 64, 128], P(None, 'wafer', ('section', 'sub')), may hold values from 0 to 127, as said below
- counts: int32 [1, 64, 8], P(None, 'wafer', ('section', 'sub')), may hold values from 2 to 16
Outputs:
- sky_map: float32 [8192], P(('wafer', 'sub'))
The draws below stay inside these ranges and needn't reach their ends.
Inputs may be any that keep to these rules, and one draw needn't show every extreme that they name: `hitlist`: for each micro-batch, source device and tile, the live slots name distinct blocks of that source, and no block is named by live slots of two tiles; in each micro-batch exactly one tile has a full hit list (all 16 slots live) from every source device.
All inputs are finite; a program needn't handle non-finite values.
Results may differ from the reference program's by a relative error of at most 0.0003.
Values sent between devices are 32-bit elements; how exact they have to be, the bound alone decides.
A program may use at most 64 MiB of HBM per device.

```python
import math
import jax
import jax.numpy as jnp
import numpy as np
from jax import lax

TEMPL = 64
DET_W = 64
SAMP_L = 256
MB = 1
BL = 128
TILE = 512
DETS = 256
SAMPLES = 2048
OWNERS = 16
NBL = 128
CAPB = 16
HOT = 1
NPIX = 8192
N_SECTION = 2
N_WAFER = 4
N_SUB = 4


def hit_plan(key):
    block_count = N_SECTION * N_SUB
    key_hot = jax.random.fold_in(key, 101)
    key_other = jax.random.fold_in(key, 102)
    key_mult = jax.random.fold_in(key, 103)
    key_shift = jax.random.fold_in(key, 104)
    ranks = jax.vmap(lambda subkey: jax.random.permutation(subkey, OWNERS))(jax.random.split(key_hot, MB))
    hot_mask = ranks < HOT
    lowest = max(1, CAPB // 8)
    highest = max(lowest, 7 * CAPB // 16)
    others = jax.random.randint(key_other, (MB, N_WAFER, block_count, OWNERS), lowest, highest + 1)
    live_counts = jnp.where(hot_mask[:, None, None, :], CAPB, others).astype(jnp.int32)
    offsets = jnp.cumsum(live_counts, axis=-1) - live_counts
    slot_ids = jnp.arange(CAPB, dtype=jnp.int32)
    position = (offsets[..., None] + slot_ids) % NBL
    multiplier = 2 * jax.random.randint(key_mult, (MB, N_WAFER, block_count, 1, 1), 0, NBL // 2) + 1
    shift_by = jax.random.randint(key_shift, (MB, N_WAFER, block_count, 1, 1), 0, NBL)
    block_ids = (multiplier * position + shift_by) % NBL
    count_out = live_counts.transpose(0, 1, 3, 2).reshape(MB, N_WAFER * OWNERS, block_count)
    hit_out = block_ids.transpose(0, 1, 3, 2, 4).reshape(MB, N_WAFER * OWNERS, block_count * CAPB)
    return (hit_out.astype(jnp.int32), count_out.astype(jnp.int32))


def draw_hitlist(key, part):
    return hit_plan(key)[0]


def draw_counts(key, part):
    return hit_plan(key)[1]


def draw_templates(key, part):
    rows = N_WAFER * TEMPL
    key_noise = jax.random.fold_in(key, 201)
    key_scale = jax.random.fold_in(key, 202)
    key_mix = jax.random.fold_in(key, 203)
    key_common = jax.random.fold_in(key, 204)
    noise = jax.random.normal(key_noise, (MB, rows, SAMPLES), jnp.float32)
    share = 0.7
    scale = jnp.exp(jax.random.uniform(key_scale, (MB, rows, 1), jnp.float32, jnp.log(0.3), jnp.log(3.0)))
    mix = jax.random.normal(key_mix, (MB, rows, 1), jnp.float32) * share
    common = jax.random.normal(key_common, (MB, N_WAFER, 1, SAMPLES), jnp.float32)
    common = jnp.broadcast_to(common, (MB, N_WAFER, TEMPL, SAMPLES)).reshape(MB, rows, SAMPLES)
    return scale * noise + mix * common


def place_ends(result, key, least, largest):
    longest = result.shape.index(max(result.shape))
    spots = []
    for shift in (0, 1):
        where = [jax.random.randint(jax.random.fold_in(key, axis), (), 0, length) for axis, length in enumerate(result.shape)]
        where[longest] = (where[longest] + shift) % result.shape[longest]
        spots.append(tuple(where))
    return result.at[spots[0]].set(least).at[spots[1]].set(largest)


def block_levels(rng, dims, shards, smallest, top_value):
    def one(dim, shards_of):
        steps = jax.random.uniform(jax.random.fold_in(jax.random.fold_in(rng, 6), dim), (shards_of,), jnp.float32, smallest / len(shards), top_value / len(shards))
        return jnp.repeat(jnp.exp(steps), dims[dim] // shards_of).reshape((-1,) + (1,) * (len(dims) - dim - 1))

    level = one(*shards[0])
    for cut in shards[1:]:
        level = level * one(*cut)
    return level


def cumulative_ranks(amount, slope):
    weights = [(1 << 20) // math.isqrt(standing ** slope) + 1 for standing in range(1, amount + 1)]
    scale = 1 + sum(weights) // (1 << 30)
    return np.cumsum(np.array([max(1, weight // scale) for weight in weights]))


def skewed_ids(own_key, shape, amount, slope):
    grid = cumulative_ranks(amount, slope)
    lot = jax.random.randint(jax.random.fold_in(own_key, 1), shape, 0, int(grid[amount - 1]))
    rank = jnp.searchsorted(jnp.asarray(grid, jnp.int32), lot, side="right")
    return jax.random.permutation(jax.random.fold_in(own_key, 2), amount)[rank].astype(jnp.int32)


def scatter_about(rng, dims, deviation, most, pieces=(), held_as=jnp.bfloat16):
    array = jax.random.normal(rng, dims, jnp.float32) * deviation
    if len(pieces) > 0:
        array = block_levels(rng, dims, pieces, -0.22, 0.18) * array
    return jnp.clip(array, min=-most, max=most).astype(held_as)


def setup_inputs(seed: int = 0) -> dict:
    key_of = jax.random.split(jax.random.key(seed), 7)
    return {
        "tod": scatter_about(key_of[0], (MB, DETS, SAMPLES), 1.0, 6.0, ((1, 4), (2, 8)), jnp.float32),
        "templates": draw_templates(jax.random.fold_in(key_of[6], 71), 0),
        "det_weight": jnp.clip(jnp.exp(math.log(3.0) - 2.3025851 * jax.random.uniform(key_of[2], (DETS,), jnp.float32) ** block_levels(key_of[2], (DETS,), ((0, 4),), -0.2, 0.2)), 0.3, 3.0),
        "pixel": place_ends(skewed_ids(key_of[3], (MB, DETS, SAMPLES), TILE, 3), jax.random.fold_in(key_of[3], 3), 0, TILE - 1).astype(jnp.int32),
        "hitlist": draw_hitlist(jax.random.fold_in(key_of[6], 71), 0),
        "counts": draw_counts(jax.random.fold_in(key_of[6], 71), 0),
    }


def pick_rows(source_rows, row_index):
    return source_rows[row_index]

def solve_fit(factor_one, proj_one):
    return jax.scipy.linalg.cho_solve((factor_one, True), proj_one)

def reference(tod, templates, det_weight, pixel, hitlist, counts):
    block_count = N_SECTION * N_SUB
    per_det = SAMP_L // BL
    owner_base = jnp.arange(OWNERS, dtype=jnp.int32) * TILE
    slot_ids = jnp.arange(CAPB, dtype=jnp.int32)
    num_map = jnp.zeros((NPIX,), jnp.float32)
    wgt_map = jnp.zeros((NPIX,), jnp.float32)
    block_weight = jnp.repeat(det_weight.reshape(N_WAFER, DET_W), per_det, axis=1)
    for batch_index in range(MB):
        streams = tod[batch_index].reshape(N_WAFER, DET_W, SAMPLES)
        modes = templates[batch_index].reshape(N_WAFER, TEMPL, SAMPLES)
        gram = jnp.einsum('wks,wls->wkl', modes, modes, precision=lax.Precision.HIGHEST)
        proj = jnp.einsum('wks,wds->wkd', modes, streams, precision=lax.Precision.HIGHEST)
        factor = jnp.linalg.cholesky(gram)
        coef = jax.vmap(solve_fit)(factor, proj)
        filtered = streams - jnp.einsum('wkd,wks->wds', coef, modes, precision=lax.Precision.HIGHEST)
        weighted = filtered * det_weight.reshape(N_WAFER, DET_W, 1)
        value_blocks = weighted.reshape(N_WAFER, DET_W, block_count, per_det, BL)
        value_blocks = value_blocks.transpose(0, 2, 1, 3, 4).reshape(N_WAFER, block_count, NBL, BL)
        pixel_blocks = pixel[batch_index].reshape(N_WAFER, DET_W, block_count, per_det, BL)
        pixel_blocks = pixel_blocks.transpose(0, 2, 1, 3, 4).reshape(N_WAFER, block_count, NBL, BL)
        hit_rows = hitlist[batch_index].reshape(N_WAFER, OWNERS, block_count, CAPB).transpose(0, 2, 1, 3)
        live_counts = counts[batch_index].reshape(N_WAFER, OWNERS, block_count).transpose(0, 2, 1)

        def one_wafer(carry, inputs_now):
            num_now, wgt_now = carry
            wafer_values, wafer_pixels, wafer_weight, wafer_hits, wafer_counts = inputs_now
            live_slots = slot_ids[None, None, :] < wafer_counts[:, :, None]
            values = jax.vmap(pick_rows)(wafer_values, wafer_hits)
            pixels = jax.vmap(pick_rows)(wafer_pixels, wafer_hits)
            values = jnp.where(live_slots[..., None], values, 0.0)
            weights = jnp.where(live_slots, wafer_weight[wafer_hits], 0.0)
            weights = jnp.broadcast_to(weights[..., None], values.shape)
            keys = (owner_base[None, :, None, None] + pixels).astype(jnp.int32)
            num_now = num_now + jax.ops.segment_sum(values.reshape(-1), keys.reshape(-1), num_segments=NPIX)
            wgt_now = wgt_now + jax.ops.segment_sum(weights.reshape(-1), keys.reshape(-1), num_segments=NPIX)
            return ((num_now, wgt_now), None)
        (num_map, wgt_map), unused = lax.scan(one_wafer, (num_map, wgt_map), (value_blocks, pixel_blocks, block_weight, hit_rows, live_counts))
    return num_map / jnp.maximum(wgt_map, 1.0)
```

```python
import functools

import jax
import jax.numpy as jnp
from jax import lax
from jax.experimental import pallas as pl
from jax.experimental.pallas import tpu as pltpu
from jax.sharding import PartitionSpec as P

BL = 128
TILE = 512
LANES = 128
MESH = pl.DeviceIdType.MESH
HIGHEST = lax.Precision.HIGHEST


def solve_augmented(blocks, unknowns):
    row = lax.broadcasted_iota(jnp.int32, blocks[0].shape, 0)
    shape = blocks[0].shape
    for kb in range(unknowns // 8):
        cols = [
            [jnp.broadcast_to(b[:, kb * 8 + t : kb * 8 + t + 1], shape) for t in range(8)]
            for b in blocks
        ]
        rows = blocks[kb]
        c = list(cols[kb])
        for t in range(8):
            inv = 1.0 / c[t][t : t + 1, :]
            scaled = rows[t : t + 1, :] * inv
            rows = jnp.where(row == t, scaled, rows - c[t] * scaled)
            for s in range(t + 1, 8):
                m = c[s][t : t + 1, :] * inv
                c[s] = jnp.where(row == t, m, c[s] - c[t] * m)
        for rb in range(len(blocks)):
            if rb == kb:
                continue
            b = blocks[rb]
            for t in range(8):
                b = b - cols[rb][t] * rows[t : t + 1, :]
            blocks[rb] = b
        blocks[kb] = rows
    return blocks


def kernel(
    sizes,
    tod_ref,
    tmpl_ref,
    weight_ref,
    pixel_ref,
    hit_ref,
    count_ref,
    out_ref,
    aug,
    red_in,
    full,
    upper,
    lower,
    vals_hi,
    vals_lo,
    num_out,
    wgt_out,
    num_in,
    wgt_in,
    red_send,
    red_recv,
    all_send,
    all_recv,
    wgt_send,
    wgt_recv,
    num_send,
    num_recv,
):
    n_sec, n_waf, n_sub = sizes
    group = n_sec * n_sub
    total = group * n_waf
    sec, waf, sub = (lax.axis_index(a) for a in ("section", "wafer", "sub"))
    me_group = sec * n_sub + sub
    me = (sec * n_waf + waf) * n_sub + sub
    my_tile = waf * n_sub + sub
    dets, samp = tod_ref.shape
    templ = tmpl_ref.shape[0]
    owners, slots = hit_ref.shape
    per_det = samp // BL
    up_count = TILE // LANES
    rows_up = owners * up_count
    part = templ // group

    def group_peer(step):
        g = lax.rem(me_group + step, group)
        return g, (g // n_sub, waf, lax.rem(g, n_sub))

    def any_peer(step):
        g = lax.rem(me + step, total)
        dev = (g // (n_waf * n_sub), lax.rem(g // n_sub, n_waf), lax.rem(g, n_sub))
        return lax.rem(g, n_waf * n_sub), dev

    barrier = pltpu.get_barrier_semaphore()

    @pl.loop(1, total)
    def _(step):
        pl.semaphore_signal(barrier, inc=1, device_id=any_peer(step)[1], device_id_type=MESH)

    modes = tmpl_ref[...]
    both = jnp.concatenate([modes, tod_ref[...]], axis=0)
    local = lax.dot_general(
        modes, both, (((1,), (1,)), ((), ())), precision=HIGHEST,
        preferred_element_type=jnp.float32,
    )
    aug[...] = local.reshape(aug.shape)
    pl.semaphore_wait(barrier, total - 1)

    @pl.loop(1, group)
    def _(step):
        g, dev = group_peer(step)
        pltpu.make_async_remote_copy(
            src_ref=aug.at[g], dst_ref=red_in.at[step - 1],
            send_sem=red_send, recv_sem=red_recv, device_id=dev, device_id_type=MESH,
        ).start()

    nblk = dets * per_det
    hits = hit_ref[...]
    live = count_ref[...]
    blk = lax.broadcasted_iota(jnp.int32, (owners, nblk), 1)
    owner_id = lax.broadcasted_iota(jnp.int32, (owners, nblk), 0) + 1
    named = jnp.zeros((owners, nblk), jnp.int32)
    for j in range(slots):
        named = jnp.where((hits[:, j : j + 1] == blk) & (live > j), owner_id, named)
    tile_row = jnp.sum(named.astype(jnp.float32), axis=0, keepdims=True)
    tile_row = jnp.broadcast_to(tile_row, (BL, nblk))
    pick_d = lax.broadcasted_iota(jnp.int32, (dets, nblk), 0)
    pick_b = lax.broadcasted_iota(jnp.int32, (dets, nblk), 1)
    pixels = pixel_ref[...]
    tiles = []
    for h in range(per_det):
        pick = (pick_b == pick_d * per_det + h).astype(jnp.float32)
        tiles.append(
            lax.dot_general(
                pick, tile_row, (((1,), (1,)), ((), ())), precision=HIGHEST,
                preferred_element_type=jnp.float32,
            )
        )
    tile = jnp.concatenate(tiles, axis=1).astype(jnp.int32) - 1
    up = tile * up_count + lax.shift_right_logical(pixels, 7)
    upper[...] = jnp.where(tile < 0, -1, up)
    lower[...] = jnp.bitwise_and(pixels, LANES - 1)

    eye_r = lax.broadcasted_iota(jnp.int32, (dets, dets), 0)
    eye_c = lax.broadcasted_iota(jnp.int32, (dets, dets), 1)
    weight = jnp.sum(
        jnp.where(eye_r == eye_c, jnp.broadcast_to(weight_ref[...], (dets, dets)), 0.0),
        axis=1, keepdims=True,
    )
    weight = jnp.broadcast_to(weight, (dets, samp))

    def split(values):
        hi = values.astype(jnp.bfloat16).astype(jnp.float32)
        vals_hi[...] = hi
        vals_lo[...] = values - hi

    def bin_all():
        up_iota = lax.broadcasted_iota(jnp.int32, (rows_up, samp), 0)
        low_iota = lax.broadcasted_iota(jnp.int32, (LANES, samp), 0)

        def body(c, acc):
            d0 = pl.multiple_of(c * 8, 8)
            u8 = upper[pl.ds(d0, 8), :]
            l8 = lower[pl.ds(d0, 8), :]
            h8 = vals_hi[pl.ds(d0, 8), :]
            o8 = vals_lo[pl.ds(d0, 8), :]
            lhs, rhs = [], []
            for i in range(8):
                hot = u8[i : i + 1, :] == up_iota
                a_hi = jnp.where(hot, h8[i : i + 1, :], 0.0).astype(jnp.bfloat16)
                a_lo = jnp.where(hot, o8[i : i + 1, :], 0.0).astype(jnp.bfloat16)
                lhs.append(jnp.concatenate([a_hi, a_lo], axis=0))
                rhs.append((l8[i : i + 1, :] == low_iota).astype(jnp.float32).astype(jnp.bfloat16))
            return acc + lax.dot_general(
                jnp.concatenate(lhs, axis=1), jnp.concatenate(rhs, axis=1),
                (((1,), (1,)), ((), ())), preferred_element_type=jnp.float32,
            )

        acc = lax.fori_loop(0, dets // 8, body, jnp.zeros((2 * rows_up, LANES), jnp.float32))
        return (acc[:rows_up] + acc[rows_up:]).reshape(owners, up_count, LANES)

    def send_tiles(out, landing, send_sem, recv_sem):
        @pl.loop(1, total)
        def _(step):
            o, dev = any_peer(step)
            pltpu.make_async_remote_copy(
                src_ref=out.at[o], dst_ref=landing.at[step - 1],
                send_sem=send_sem, recv_sem=recv_sem, device_id=dev, device_id_type=MESH,
            ).start()

    def wait_all(ref, sem):
        pltpu.make_async_copy(ref, ref, sem).wait()

    wait_all(red_in, red_recv)
    mine = aug[me_group]
    for step in range(group - 1):
        mine = mine + red_in[step]
    full[me_group] = mine

    @pl.loop(1, group)
    def _(step):
        g, dev = group_peer(step)
        pltpu.make_async_remote_copy(
            src_ref=full.at[me_group], dst_ref=full.at[me_group],
            send_sem=all_send, recv_sem=all_recv, device_id=dev, device_id_type=MESH,
        ).start()

    split(weight)
    wgt_out[...] = bin_all()
    send_tiles(wgt_out, wgt_in, wgt_send, wgt_recv)
    wait_all(red_in, all_recv)

    system = full[...].reshape(templ, templ + dets)
    blocks = [system[8 * b : 8 * b + 8, :] for b in range(templ // 8)]
    coef = jnp.concatenate(solve_augmented(blocks, templ), axis=0)[:, templ:]
    removed = lax.dot_general(
        coef, tmpl_ref[...], (((0,), (0,)), ((), ())), precision=HIGHEST,
        preferred_element_type=jnp.float32,
    )
    split((tod_ref[...] - removed) * weight)
    num_out[...] = bin_all()
    send_tiles(num_out, num_in, num_send, num_recv)

    wait_all(wgt_in, wgt_recv)
    wgt = wgt_out[my_tile] + jnp.sum(wgt_in[...], axis=0)
    wait_all(num_in, num_recv)
    num = num_out[my_tile] + jnp.sum(num_in[...], axis=0)
    out_ref[...] = num / jnp.maximum(wgt, 1.0)

    wait_all(red_in, red_send)
    wait_all(red_in, all_send)
    wait_all(wgt_in, wgt_send)
    wait_all(num_in, num_send)


def shards(sizes, tod, templates, det_weight, pixel, hitlist, counts):
    n_sec, n_waf, n_sub = sizes
    group = n_sec * n_sub
    total = group * n_waf
    dets, samp = tod.shape[1:]
    templ = templates.shape[1]
    owners = hitlist.shape[1]
    part = templ // group
    up_count = TILE // LANES
    vmem = pl.BlockSpec(memory_space=pltpu.VMEM)
    f32, i32 = jnp.float32, jnp.int32
    wide = templ + dets
    out = pl.pallas_call(
        functools.partial(kernel, sizes),
        out_shape=jax.ShapeDtypeStruct((up_count, LANES), f32),
        in_specs=[vmem] * 6,
        out_specs=vmem,
        scratch_shapes=[
            pltpu.VMEM((group, part, wide), f32),
            pltpu.VMEM((group - 1, part, wide), f32),
            pltpu.VMEM((group, part, wide), f32),
            pltpu.VMEM((dets, samp), i32),
            pltpu.VMEM((dets, samp), i32),
            pltpu.VMEM((dets, samp), f32),
            pltpu.VMEM((dets, samp), f32),
            pltpu.VMEM((owners, up_count, LANES), f32),
            pltpu.VMEM((owners, up_count, LANES), f32),
            pltpu.VMEM((total - 1, up_count, LANES), f32),
            pltpu.VMEM((total - 1, up_count, LANES), f32),
        ]
        + [pltpu.SemaphoreType.DMA] * 8,
        compiler_params=pltpu.CompilerParams(
            collective_id=0, has_side_effects=True, vmem_limit_bytes=32 * 1024 * 1024
        ),
    )(tod[0], templates[0], det_weight[None, :], pixel[0], hitlist[0], counts[0])
    return out.reshape(-1)


def solution(mesh):
    sizes = tuple(mesh.shape[a] for a in ("section", "wafer", "sub"))
    placed = (
        P(None, "wafer", ("section", "sub")),
        P(None, "wafer", ("section", "sub")),
        P("wafer"),
        P(None, "wafer", ("section", "sub")),
        P(None, "wafer", ("section", "sub")),
        P(None, "wafer", ("section", "sub")),
    )
    return jax.shard_map(
        functools.partial(shards, sizes), mesh=mesh, in_specs=placed,
        out_specs=P(("wafer", "sub")), check_vma=False,
    )
```

```python
import functools

import jax
import jax.numpy as jnp
from jax import lax
from jax.experimental import pallas as pl
from jax.experimental.pallas import tpu as pltpu
from jax.sharding import PartitionSpec as P

BL = 128
TILE = 512
LANES = 128
MESH = pl.DeviceIdType.MESH
HIGHEST = lax.Precision.HIGHEST


def solve_augmented(blocks, unknowns):
    row = lax.broadcasted_iota(jnp.int32, blocks[0].shape, 0)
    shape = blocks[0].shape
    for kb in range(unknowns // 8):
        cols = [
            [jnp.broadcast_to(b[:, kb * 8 + t : kb * 8 + t + 1], shape) for t in range(8)]
            for b in blocks
        ]
        rows = blocks[kb]
        c = list(cols[kb])
        for t in range(8):
            inv = 1.0 / c[t][t : t + 1, :]
            scaled = rows[t : t + 1, :] * inv
            rows = jnp.where(row == t, scaled, rows - c[t] * scaled)
            for s in range(t + 1, 8):
                m = c[s][t : t + 1, :] * inv
                c[s] = jnp.where(row == t, m, c[s] - c[t] * m)
        for rb in range(len(blocks)):
            if rb == kb:
                continue
            b = blocks[rb]
            for t in range(8):
                b = b - cols[rb][t] * rows[t : t + 1, :]
            blocks[rb] = b
        blocks[kb] = rows
    return blocks


def kernel(
    sizes,
    tod_hbm,
    tmpl_hbm,
    weight_hbm,
    pixel_hbm,
    hit_hbm,
    count_hbm,
    out_ref,
    tod_ref,
    tmpl_ref,
    weight_ref,
    pixel_ref,
    hit_ref,
    count_ref,
    aug,
    red_in,
    full,
    upper,
    lower,
    vals_hi,
    vals_lo,
    num_out,
    wgt_out,
    num_in,
    wgt_in,
    red_send,
    red_recv,
    all_send,
    all_recv,
    wgt_send,
    wgt_recv,
    num_send,
    num_recv,
    load_sems,
):
    n_sec, n_waf, n_sub = sizes
    group = n_sec * n_sub
    total = group * n_waf
    sec, waf, sub = (lax.axis_index(a) for a in ("section", "wafer", "sub"))
    me_group = sec * n_sub + sub
    me = (sec * n_waf + waf) * n_sub + sub
    my_tile = waf * n_sub + sub
    dets, samp = tod_ref.shape
    templ = tmpl_ref.shape[0]
    owners, slots = hit_ref.shape
    per_det = samp // BL
    up_count = TILE // LANES
    rows_up = owners * up_count
    part = templ // group

    def shifted(index, step, size):
        if size & (size - 1) == 0:
            return jnp.bitwise_xor(index, step)
        return lax.rem(index + step, size)

    def cut(index, size):
        if size & (size - 1) == 0:
            shift = size.bit_length() - 1
            return lax.shift_right_logical(index, shift), jnp.bitwise_and(index, size - 1)
        return index // size, lax.rem(index, size)

    def group_peer(step):
        g = shifted(me_group, step, group)
        s, z = cut(g, n_sub)
        return g, (s, waf, z)

    def any_peer(step):
        g = shifted(me, step, total)
        s, o = cut(g, n_waf * n_sub)
        w, z = cut(o, n_sub)
        return o, (s, w, z)

    def for_peers(size, body):
        if size <= 32:
            for step in range(1, size):
                body(jnp.int32(step))
        else:
            pl.loop(1, size)(body)

    loads = [
        pltpu.make_async_copy(src, dst, load_sems.at[i])
        for i, (src, dst) in enumerate(
            (
                (tmpl_hbm, tmpl_ref),
                (tod_hbm, tod_ref),
                (hit_hbm, hit_ref),
                (count_hbm, count_ref),
                (pixel_hbm, pixel_ref),
                (weight_hbm, weight_ref),
            )
        )
    ]
    for load in loads:
        load.start()
    barrier = pltpu.get_barrier_semaphore()

    def greet(step):
        pl.semaphore_signal(barrier, inc=1, device_id=any_peer(step)[1], device_id_type=MESH)

    for_peers(total, greet)

    loads[0].wait()
    loads[1].wait()
    modes = tmpl_ref[...]
    both = jnp.concatenate([modes, tod_ref[...]], axis=0)
    local = lax.dot_general(
        modes, both, (((1,), (1,)), ((), ())), precision=HIGHEST,
        preferred_element_type=jnp.float32,
    )
    aug[...] = local.reshape(aug.shape)
    pl.semaphore_wait(barrier, total - 1)

    def send_rows(step):
        g, dev = group_peer(step)
        pltpu.make_async_remote_copy(
            src_ref=aug.at[g], dst_ref=red_in.at[step - 1],
            send_sem=red_send, recv_sem=red_recv, device_id=dev, device_id_type=MESH,
        ).start()

    for_peers(group, send_rows)

    for load in loads[2:]:
        load.wait()
    nblk = dets * per_det
    hits = hit_ref[...]
    live = jnp.sum(
        jnp.where(
            lax.broadcasted_iota(jnp.int32, (owners, owners), 0)
            == lax.broadcasted_iota(jnp.int32, (owners, owners), 1),
            jnp.broadcast_to(count_ref[...].astype(jnp.float32), (owners, owners)),
            0.0,
        ),
        axis=1, keepdims=True,
    ).astype(jnp.int32)
    blk = lax.broadcasted_iota(jnp.int32, (owners, nblk), 1)
    owner_id = lax.broadcasted_iota(jnp.int32, (owners, nblk), 0) + 1
    named = jnp.zeros((owners, nblk), jnp.int32)
    for j in range(slots):
        named = jnp.where((hits[:, j : j + 1] == blk) & (live > j), owner_id, named)
    tile_row = jnp.sum(named.astype(jnp.float32), axis=0, keepdims=True)
    tile_row = jnp.broadcast_to(tile_row, (BL, nblk))
    pick_d = lax.broadcasted_iota(jnp.int32, (dets, nblk), 0)
    pick_b = lax.broadcasted_iota(jnp.int32, (dets, nblk), 1)
    pixels = pixel_ref[...]
    tiles = []
    for h in range(per_det):
        pick = (pick_b == pick_d * per_det + h).astype(jnp.float32)
        tiles.append(
            lax.dot_general(
                pick, tile_row, (((1,), (1,)), ((), ())), precision=HIGHEST,
                preferred_element_type=jnp.float32,
            )
        )
    tile = jnp.concatenate(tiles, axis=1).astype(jnp.int32) - 1
    up = tile * up_count + lax.shift_right_logical(pixels, 7)
    upper[...] = jnp.where(tile < 0, -1, up)
    lower[...] = jnp.bitwise_and(pixels, LANES - 1)

    eye_r = lax.broadcasted_iota(jnp.int32, (dets, dets), 0)
    eye_c = lax.broadcasted_iota(jnp.int32, (dets, dets), 1)
    weight = jnp.sum(
        jnp.where(eye_r == eye_c, jnp.broadcast_to(weight_ref[...], (dets, dets)), 0.0),
        axis=1, keepdims=True,
    )
    weight = jnp.broadcast_to(weight, (dets, samp))

    def split(values):
        hi = values.astype(jnp.bfloat16).astype(jnp.float32)
        vals_hi[...] = hi
        vals_lo[...] = values - hi

    def bin_all():
        up_iota = lax.broadcasted_iota(jnp.int32, (rows_up, samp), 0)
        low_iota = lax.broadcasted_iota(jnp.int32, (LANES, samp), 0)

        def body(c, acc):
            d0 = pl.multiple_of(c * 8, 8)
            u8 = upper[pl.ds(d0, 8), :]
            l8 = lower[pl.ds(d0, 8), :]
            h8 = vals_hi[pl.ds(d0, 8), :]
            o8 = vals_lo[pl.ds(d0, 8), :]
            lhs, rhs = [], []
            for i in range(8):
                hot = u8[i : i + 1, :] == up_iota
                a_hi = jnp.where(hot, h8[i : i + 1, :], 0.0).astype(jnp.bfloat16)
                a_lo = jnp.where(hot, o8[i : i + 1, :], 0.0).astype(jnp.bfloat16)
                lhs.append(jnp.concatenate([a_hi, a_lo], axis=0))
                rhs.append((l8[i : i + 1, :] == low_iota).astype(jnp.float32).astype(jnp.bfloat16))
            return acc + lax.dot_general(
                jnp.concatenate(lhs, axis=1), jnp.concatenate(rhs, axis=1),
                (((1,), (1,)), ((), ())), preferred_element_type=jnp.float32,
            )

        acc = lax.fori_loop(0, dets // 8, body, jnp.zeros((2 * rows_up, LANES), jnp.float32))
        return (acc[:rows_up] + acc[rows_up:]).reshape(owners, up_count, LANES)

    def send_tiles(out, landing, send_sem, recv_sem):
        def send(step):
            o, dev = any_peer(step)
            pltpu.make_async_remote_copy(
                src_ref=out.at[o], dst_ref=landing.at[step - 1],
                send_sem=send_sem, recv_sem=recv_sem, device_id=dev, device_id_type=MESH,
            ).start()

        for_peers(total, send)

    def wait_all(ref, sem):
        pltpu.make_async_copy(ref, ref, sem).wait()

    wait_all(red_in, red_recv)
    mine = aug[me_group]
    for step in range(group - 1):
        mine = mine + red_in[step]
    full[me_group] = mine

    def send_sums(step):
        g, dev = group_peer(step)
        pltpu.make_async_remote_copy(
            src_ref=full.at[me_group], dst_ref=full.at[me_group],
            send_sem=all_send, recv_sem=all_recv, device_id=dev, device_id_type=MESH,
        ).start()

    for_peers(group, send_sums)

    split(weight)
    wgt_out[...] = bin_all()
    send_tiles(wgt_out, wgt_in, wgt_send, wgt_recv)
    wait_all(red_in, all_recv)

    system = full[...].reshape(templ, templ + dets)
    blocks = [system[8 * b : 8 * b + 8, :] for b in range(templ // 8)]
    coef = jnp.concatenate(solve_augmented(blocks, templ), axis=0)[:, templ:]
    removed = lax.dot_general(
        coef, tmpl_ref[...], (((0,), (0,)), ((), ())), precision=HIGHEST,
        preferred_element_type=jnp.float32,
    )
    split((tod_ref[...] - removed) * weight)
    num_out[...] = bin_all()
    send_tiles(num_out, num_in, num_send, num_recv)

    wait_all(wgt_in, wgt_recv)
    wgt = wgt_out[my_tile] + jnp.sum(wgt_in[...], axis=0)
    wait_all(num_in, num_recv)
    num = num_out[my_tile] + jnp.sum(num_in[...], axis=0)
    out_ref[...] = num / jnp.maximum(wgt, 1.0)

    wait_all(red_in, red_send)
    wait_all(red_in, all_send)
    wait_all(wgt_in, wgt_send)
    wait_all(num_in, num_send)


def shards(sizes, tod, templates, det_weight, pixel, hitlist, counts):
    n_sec, n_waf, n_sub = sizes
    group = n_sec * n_sub
    total = group * n_waf
    dets, samp = tod.shape[1:]
    templ = templates.shape[1]
    owners, slots = hitlist.shape[1:]
    part = templ // group
    up_count = TILE // LANES
    vmem = pl.BlockSpec(memory_space=pltpu.VMEM)
    f32, i32 = jnp.float32, jnp.int32
    wide = templ + dets
    out = pl.pallas_call(
        functools.partial(kernel, sizes),
        out_shape=jax.ShapeDtypeStruct((up_count, LANES), f32),
        in_specs=[pl.BlockSpec(memory_space=pltpu.HBM)] * 6,
        out_specs=vmem,
        scratch_shapes=[
            pltpu.VMEM((dets, samp), f32),
            pltpu.VMEM((templ, samp), f32),
            pltpu.VMEM((1, dets), f32),
            pltpu.VMEM((dets, samp), i32),
            pltpu.VMEM((owners, slots), i32),
            pltpu.VMEM((1, owners), i32),
            pltpu.VMEM((group, part, wide), f32),
            pltpu.VMEM((group - 1, part, wide), f32),
            pltpu.VMEM((group, part, wide), f32),
            pltpu.VMEM((dets, samp), i32),
            pltpu.VMEM((dets, samp), i32),
            pltpu.VMEM((dets, samp), f32),
            pltpu.VMEM((dets, samp), f32),
            pltpu.VMEM((owners, up_count, LANES), f32),
            pltpu.VMEM((owners, up_count, LANES), f32),
            pltpu.VMEM((total - 1, up_count, LANES), f32),
            pltpu.VMEM((total - 1, up_count, LANES), f32),
        ]
        + [pltpu.SemaphoreType.DMA] * 8
        + [pltpu.SemaphoreType.DMA((6,))],
        compiler_params=pltpu.CompilerParams(
            collective_id=0, has_side_effects=True, vmem_limit_bytes=63 * 1024 * 1024
        ),
    )(tod[0], templates[0], det_weight[None, :], pixel[0], hitlist[0], counts[0].T)
    return out.reshape(-1)


def solution(mesh):
    sizes = tuple(mesh.shape[a] for a in ("section", "wafer", "sub"))
    placed = (
        P(None, "wafer", ("section", "sub")),
        P(None, "wafer", ("section", "sub")),
        P("wafer"),
        P(None, "wafer", ("section", "sub")),
        P(None, "wafer", ("section", "sub")),
        P(None, "wafer", ("section", "sub")),
    )
    return jax.shard_map(
        functools.partial(shards, sizes), mesh=mesh, in_specs=placed,
        out_specs=P(("wafer", "sub")), check_vma=False,
    )
```

```python
import functools

import jax
import jax.numpy as jnp
from jax import lax
from jax.experimental import pallas as pl
from jax.experimental.pallas import tpu as pltpu
from jax.sharding import PartitionSpec as P

BL = 128
TILE = 512
LANES = 128
MESH = pl.DeviceIdType.MESH
HIGHEST = lax.Precision.HIGHEST


def solve_augmented(blocks, unknowns):
    row = lax.broadcasted_iota(jnp.int32, blocks[0].shape, 0)
    shape = blocks[0].shape
    for kb in range(unknowns // 8):
        cols = [
            [jnp.broadcast_to(b[:, kb * 8 + t : kb * 8 + t + 1], shape) for t in range(8)]
            for b in blocks
        ]
        rows = blocks[kb]
        c = list(cols[kb])
        for t in range(8):
            inv = 1.0 / c[t][t : t + 1, :]
            scaled = rows[t : t + 1, :] * inv
            rows = jnp.where(row == t, scaled, rows - c[t] * scaled)
            for s in range(t + 1, 8):
                m = c[s][t : t + 1, :] * inv
                c[s] = jnp.where(row == t, m, c[s] - c[t] * m)
        for rb in range(len(blocks)):
            if rb == kb:
                continue
            b = blocks[rb]
            for t in range(8):
                b = b - cols[rb][t] * rows[t : t + 1, :]
            blocks[rb] = b
        blocks[kb] = rows
    return blocks


def kernel(
    sizes,
    tod_hbm,
    tmpl_hbm,
    weight_hbm,
    pixel_hbm,
    hit_hbm,
    count_hbm,
    out_ref,
    tod_ref,
    tmpl_ref,
    weight_ref,
    pixel_ref,
    hit_ref,
    count_ref,
    aug,
    red_in,
    full,
    upper,
    lower,
    vals_hi,
    vals_lo,
    num_out,
    wgt_out,
    num_in,
    wgt_in,
    red_send,
    red_recv,
    all_send,
    all_recv,
    wgt_send,
    wgt_recv,
    num_send,
    num_recv,
    load_sems,
    low_hot,
    up_hot,
):
    n_sec, n_waf, n_sub = sizes
    group = n_sec * n_sub
    total = group * n_waf
    sec, waf, sub = (lax.axis_index(a) for a in ("section", "wafer", "sub"))
    me_group = sec * n_sub + sub
    me = (sec * n_waf + waf) * n_sub + sub
    my_tile = waf * n_sub + sub
    dets, samp = tod_ref.shape
    templ = tmpl_ref.shape[0]
    owners, slots = hit_ref.shape
    per_det = samp // BL
    up_count = TILE // LANES
    rows_up = owners * up_count
    part = templ // group

    def shifted(index, step, size):
        if size & (size - 1) == 0:
            return jnp.bitwise_xor(index, step)
        return lax.rem(index + step, size)

    def cut(index, size):
        if size & (size - 1) == 0:
            shift = size.bit_length() - 1
            return lax.shift_right_logical(index, shift), jnp.bitwise_and(index, size - 1)
        return index // size, lax.rem(index, size)

    def group_peer(step):
        g = shifted(me_group, step, group)
        s, z = cut(g, n_sub)
        return g, (s, waf, z)

    def any_peer(step):
        g = shifted(me, step, total)
        s, o = cut(g, n_waf * n_sub)
        w, z = cut(o, n_sub)
        return o, (s, w, z)

    def for_peers(size, body):
        if size <= 32:
            for step in range(1, size):
                body(jnp.int32(step))
        else:
            pl.loop(1, size)(body)

    loads = [
        pltpu.make_async_copy(src, dst, load_sems.at[i])
        for i, (src, dst) in enumerate(
            (
                (tmpl_hbm, tmpl_ref),
                (tod_hbm, tod_ref),
                (hit_hbm, hit_ref),
                (count_hbm, count_ref),
                (pixel_hbm, pixel_ref),
                (weight_hbm, weight_ref),
            )
        )
    ]
    for load in loads:
        load.start()
    barrier = pltpu.get_barrier_semaphore()

    def greet(step):
        pl.semaphore_signal(barrier, inc=1, device_id=any_peer(step)[1], device_id_type=MESH)

    for_peers(total, greet)

    loads[0].wait()
    loads[1].wait()
    modes = tmpl_ref[...]
    both = jnp.concatenate([modes, tod_ref[...]], axis=0)
    local = lax.dot_general(
        modes, both, (((1,), (1,)), ((), ())), precision=HIGHEST,
        preferred_element_type=jnp.float32,
    )
    aug[...] = local.reshape(aug.shape)
    pl.semaphore_wait(barrier, total - 1)

    def send_rows(step):
        g, dev = group_peer(step)
        pltpu.make_async_remote_copy(
            src_ref=aug.at[g], dst_ref=red_in.at[step - 1],
            send_sem=red_send, recv_sem=red_recv, device_id=dev, device_id_type=MESH,
        ).start()

    for_peers(group, send_rows)

    for load in loads[2:]:
        load.wait()
    nblk = dets * per_det
    hits = hit_ref[...]
    live = jnp.sum(
        jnp.where(
            lax.broadcasted_iota(jnp.int32, (owners, owners), 0)
            == lax.broadcasted_iota(jnp.int32, (owners, owners), 1),
            jnp.broadcast_to(count_ref[...].astype(jnp.float32), (owners, owners)),
            0.0,
        ),
        axis=1, keepdims=True,
    ).astype(jnp.int32)
    blk = lax.broadcasted_iota(jnp.int32, (owners, nblk), 1)
    owner_id = lax.broadcasted_iota(jnp.int32, (owners, nblk), 0) + 1
    named = jnp.zeros((owners, nblk), jnp.int32)
    for j in range(slots):
        named = jnp.where((hits[:, j : j + 1] == blk) & (live > j), owner_id, named)
    tile_row = jnp.sum(named.astype(jnp.float32), axis=0, keepdims=True)
    tile_row = jnp.broadcast_to(tile_row, (BL, nblk))
    pick_d = lax.broadcasted_iota(jnp.int32, (dets, nblk), 0)
    pick_b = lax.broadcasted_iota(jnp.int32, (dets, nblk), 1)
    pixels = pixel_ref[...]
    tiles = []
    for h in range(per_det):
        pick = (pick_b == pick_d * per_det + h).astype(jnp.float32)
        tiles.append(
            lax.dot_general(
                pick, tile_row, (((1,), (1,)), ((), ())), precision=HIGHEST,
                preferred_element_type=jnp.float32,
            )
        )
    tile = jnp.concatenate(tiles, axis=1).astype(jnp.int32) - 1
    up = tile * up_count + lax.shift_right_logical(pixels, 7)
    upper[...] = jnp.where(tile < 0, -1, up)
    lower[...] = jnp.bitwise_and(pixels, LANES - 1)

    eye_r = lax.broadcasted_iota(jnp.int32, (dets, dets), 0)
    eye_c = lax.broadcasted_iota(jnp.int32, (dets, dets), 1)
    weight = jnp.sum(
        jnp.where(eye_r == eye_c, jnp.broadcast_to(weight_ref[...], (dets, dets)), 0.0),
        axis=1, keepdims=True,
    )
    weight = jnp.broadcast_to(weight, (dets, samp))

    def split(values):
        hi = values.astype(jnp.bfloat16).astype(jnp.float32)
        vals_hi[...] = hi
        vals_lo[...] = values - hi

    span = 8 * samp
    up_iota = lax.broadcasted_iota(jnp.int32, (rows_up, samp), 0)
    low_iota = lax.broadcasted_iota(jnp.int32, (LANES, samp), 0)

    def build(c, carry):
        d0 = pl.multiple_of(c * 8, 8)
        u8 = upper[pl.ds(d0, 8), :]
        l8 = lower[pl.ds(d0, 8), :]
        ups, lows = [], []
        for i in range(8):
            ups.append((u8[i : i + 1, :] == up_iota).astype(jnp.float32).astype(jnp.bfloat16))
            hot = (l8[i : i + 1, :] == low_iota).astype(jnp.float32)
            lows.append(jnp.transpose(hot).astype(jnp.bfloat16))
        k0 = pl.multiple_of(c * span, span)
        low_hot[pl.ds(k0, span), :] = jnp.concatenate(lows, axis=0)
        r0 = pl.multiple_of(c * rows_up, rows_up)
        up_hot[pl.ds(r0, rows_up), :] = jnp.concatenate(ups, axis=1)
        return carry

    def bin_all():
        def spread(row):
            tile16 = jnp.broadcast_to(row, (16, samp)).astype(jnp.bfloat16)
            return jnp.concatenate([tile16] * (rows_up // 16), axis=0)

        def body(c, acc):
            d0 = pl.multiple_of(c * 8, 8)
            h8 = vals_hi[pl.ds(d0, 8), :]
            o8 = vals_lo[pl.ds(d0, 8), :]
            r0 = pl.multiple_of(c * rows_up, rows_up)
            hot = up_hot[pl.ds(r0, rows_up), :]
            his = jnp.concatenate([spread(h8[i : i + 1, :]) for i in range(8)], axis=1)
            los = jnp.concatenate([spread(o8[i : i + 1, :]) for i in range(8)], axis=1)
            k0 = pl.multiple_of(c * span, span)
            return acc + lax.dot_general(
                jnp.concatenate([hot * his, hot * los], axis=0), low_hot[pl.ds(k0, span), :],
                (((1,), (0,)), ((), ())), preferred_element_type=jnp.float32,
            )

        acc = lax.fori_loop(0, dets // 8, body, jnp.zeros((2 * rows_up, LANES), jnp.float32))
        return (acc[:rows_up] + acc[rows_up:]).reshape(owners, up_count, LANES)

    def send_tiles(out, landing, send_sem, recv_sem):
        def send(step):
            o, dev = any_peer(step)
            pltpu.make_async_remote_copy(
                src_ref=out.at[o], dst_ref=landing.at[step - 1],
                send_sem=send_sem, recv_sem=recv_sem, device_id=dev, device_id_type=MESH,
            ).start()

        for_peers(total, send)

    def wait_all(ref, sem):
        pltpu.make_async_copy(ref, ref, sem).wait()

    lax.fori_loop(0, dets // 8, build, 0)
    wait_all(red_in, red_recv)
    mine = aug[me_group]
    for step in range(group - 1):
        mine = mine + red_in[step]
    full[me_group] = mine

    def send_sums(step):
        g, dev = group_peer(step)
        pltpu.make_async_remote_copy(
            src_ref=full.at[me_group], dst_ref=full.at[me_group],
            send_sem=all_send, recv_sem=all_recv, device_id=dev, device_id_type=MESH,
        ).start()

    for_peers(group, send_sums)

    split(weight)
    wgt_out[...] = bin_all()
    send_tiles(wgt_out, wgt_in, wgt_send, wgt_recv)
    wait_all(red_in, all_recv)

    system = full[...].reshape(templ, templ + dets)
    blocks = [system[8 * b : 8 * b + 8, :] for b in range(templ // 8)]
    coef = jnp.concatenate(solve_augmented(blocks, templ), axis=0)[:, templ:]
    removed = lax.dot_general(
        coef, tmpl_ref[...], (((0,), (0,)), ((), ())), precision=HIGHEST,
        preferred_element_type=jnp.float32,
    )
    split((tod_ref[...] - removed) * weight)
    num_out[...] = bin_all()
    send_tiles(num_out, num_in, num_send, num_recv)

    wait_all(wgt_in, wgt_recv)
    wgt = wgt_out[my_tile] + jnp.sum(wgt_in[...], axis=0)
    wait_all(num_in, num_recv)
    num = num_out[my_tile] + jnp.sum(num_in[...], axis=0)
    out_ref[...] = num / jnp.maximum(wgt, 1.0)

    wait_all(red_in, red_send)
    wait_all(red_in, all_send)
    wait_all(wgt_in, wgt_send)
    wait_all(num_in, num_send)


def shards(sizes, tod, templates, det_weight, pixel, hitlist, counts):
    n_sec, n_waf, n_sub = sizes
    group = n_sec * n_sub
    total = group * n_waf
    dets, samp = tod.shape[1:]
    templ = templates.shape[1]
    owners, slots = hitlist.shape[1:]
    part = templ // group
    up_count = TILE // LANES
    vmem = pl.BlockSpec(memory_space=pltpu.VMEM)
    f32, i32 = jnp.float32, jnp.int32
    wide = templ + dets
    out = pl.pallas_call(
        functools.partial(kernel, sizes),
        out_shape=jax.ShapeDtypeStruct((up_count, LANES), f32),
        in_specs=[pl.BlockSpec(memory_space=pltpu.HBM)] * 6,
        out_specs=vmem,
        scratch_shapes=[
            pltpu.VMEM((dets, samp), f32),
            pltpu.VMEM((templ, samp), f32),
            pltpu.VMEM((1, dets), f32),
            pltpu.VMEM((dets, samp), i32),
            pltpu.VMEM((owners, slots), i32),
            pltpu.VMEM((1, owners), i32),
            pltpu.VMEM((group, part, wide), f32),
            pltpu.VMEM((group - 1, part, wide), f32),
            pltpu.VMEM((group, part, wide), f32),
            pltpu.VMEM((dets, samp), i32),
            pltpu.VMEM((dets, samp), i32),
            pltpu.VMEM((dets, samp), f32),
            pltpu.VMEM((dets, samp), f32),
            pltpu.VMEM((owners, up_count, LANES), f32),
            pltpu.VMEM((owners, up_count, LANES), f32),
            pltpu.VMEM((total - 1, up_count, LANES), f32),
            pltpu.VMEM((total - 1, up_count, LANES), f32),
        ]
        + [pltpu.SemaphoreType.DMA] * 8
        + [
            pltpu.SemaphoreType.DMA((6,)),
            pltpu.VMEM((dets * samp, LANES), jnp.bfloat16),
            pltpu.VMEM((dets // 8 * owners * up_count, 8 * samp), jnp.bfloat16),
        ],
        compiler_params=pltpu.CompilerParams(
            collective_id=0, has_side_effects=True, vmem_limit_bytes=63 * 1024 * 1024
        ),
    )(tod[0], templates[0], det_weight[None, :], pixel[0], hitlist[0], counts[0].T)
    return out.reshape(-1)


def solution(mesh):
    sizes = tuple(mesh.shape[a] for a in ("section", "wafer", "sub"))
    placed = (
        P(None, "wafer", ("section", "sub")),
        P(None, "wafer", ("section", "sub")),
        P("wafer"),
        P(None, "wafer", ("section", "sub")),
        P(None, "wafer", ("section", "sub")),
        P(None, "wafer", ("section", "sub")),
    )
    return jax.shard_map(
        functools.partial(shards, sizes), mesh=mesh, in_specs=placed,
        out_specs=P(("wafer", "sub")), check_vma=False,
    )
```
